128 devices in a mesh: grp: 4 (over x), mem: 32 (over y, z, core).
Axes of the slice: x: 4, y: 4, z: 4, core: 2. Of those that a mesh axis runs over, the one named last changes fastest.
Arguments:
- prior_trajectory: bfloat16 [128, 1024, 8, 512], P('mem', 'grp'), may hold values from -6 to 6
- measured_equivalent: bfloat16 [128, 1024, 1024], P('mem', 'grp'), may hold values from -6 to 6
- measured_datum: float32 [1024, 1024], P(('grp', 'mem')), may hold values from -10 to 10
- weighted_inverse_noise: bfloat16 [1024, 1024], P(('grp', 'mem')), may hold values from 0.049804688 to 1
- local_tallies: int32 [1024], P(('grp', 'mem')), may hold values from 1 to 1024, as said below
- device_assignment: int32 [1024], P(('grp', 'mem')), may hold values from 0 to 3, as said below
Outputs:
- analysis: bfloat16 [128, 1024, 8, 512], P(None, ('grp', 'mem'))
- slot_weights: bfloat16 [1024, 128, 128], P(('grp', 'mem'))
The draws below stay inside these ranges and needn't reach their ends.
Inputs may be any that keep to these rules, and one draw needn't show every extreme that they name: `local_tallies`: at least one block of every draw has exactly 1024 local observations. `device_assignment`: among the 32 blocks with one m (see the steps), each value is named by exactly 8 blocks; among the 8 blocks of one device, no value is named by more than 4 blocks, and every device reaches that bound.
All inputs are finite; a program needn't handle non-finite values.
Results may differ from the reference program's by a relative error of at most 0.012.
Values may be sent and summed in bfloat16 or wider, within the bound.
A program may use at most 128 MiB of HBM per device.

```python
import math
import jax
import jax.numpy as jnp
from jax import lax

MEMBER_TALLY = 128
VERTICAL_AMOUNTS = 512
TILE_VERTICALS = 8
BLK_DEV = 8
OMAX = 1024
ITERS = 12
DOMAIN_TILES = 1024
N_GRP = 4
N_MEM = 32


def joint_plan(key):
    keys = jax.random.split(key, 6)
    groups = N_GRP
    cap = BLK_DEV // 2
    perms = jax.vmap(lambda k: jax.random.permutation(k, groups))(jax.random.split(keys[0], N_MEM)).astype(jnp.int32)
    inverse = jnp.argsort(perms, axis=1).astype(jnp.int32)
    shift = jax.random.randint(keys[1], (N_MEM,), 0, groups // 2) * 2 + 1
    parity = jax.random.randint(keys[2], (N_MEM,), 0, 2)
    gidx = jnp.arange(groups, dtype=jnp.int32)
    first = inverse.T
    moved = (gidx[None, :] - shift[:, None]) % groups
    second = jnp.take_along_axis(inverse, moved.astype(jnp.int32), axis=1).T
    places = jax.vmap(lambda k: jax.random.permutation(k, BLK_DEV))(jax.random.split(keys[3], groups * N_MEM))
    places = places.reshape(groups, N_MEM, BLK_DEV).astype(jnp.int32)
    dest = jnp.where(places < cap, first[..., None], second[..., None])
    heavy = (gidx[:, None] + parity[None, :]) % 2 == 0
    big = jax.random.randint(keys[4], (groups, N_MEM, BLK_DEV), 3 * OMAX // 4, OMAX + 1)
    small = jax.random.randint(keys[5], (groups, N_MEM, BLK_DEV), 1, OMAX // 8 + 1)
    number = jnp.where(heavy[..., None], big, small)
    lead = jnp.where(heavy, OMAX, number[:, :, 0])
    number = number.at[:, :, 0].set(lead)
    return (number.reshape(-1).astype(jnp.int32), dest.reshape(-1).astype(jnp.int32))


def draw_local_tallies(key, part):
    number, dest = joint_plan(key)
    return number


def draw_device_assignment(key, part):
    number, dest = joint_plan(key)
    return dest


def level_of(key, shape, cuts, least, high):
    factor_of = 1.0
    for position, shards_of in cuts:
        heights = jax.random.uniform(jax.random.fold_in(jax.random.fold_in(key, 6), position), (shards_of,), jnp.float32, least / len(cuts), high / len(cuts))
        factor_of = factor_of * jnp.repeat(jnp.exp(heights), shape[position] // shards_of).reshape((-1,) + (1,) * (len(shape) - 1 - position))
    return factor_of


def noise(key, extent, scale, limit, pieces=(), kind=jnp.bfloat16):
    drawn = jax.random.normal(key, extent, jnp.float32) * scale
    if len(pieces) > 0:
        drawn = level_of(key, extent, pieces, -0.22, 0.18) * drawn
    return jnp.clip(drawn, min=-limit, max=limit).astype(kind)


def setup_inputs(seed: int = 0) -> dict:
    streams_of = jax.random.split(jax.random.key(seed), 7)
    prior_trajectory = noise(streams_of[0], (MEMBER_TALLY, DOMAIN_TILES, TILE_VERTICALS, VERTICAL_AMOUNTS), 1.0, 6.0, ((0, 32), (1, 4)))
    measured_equivalent = noise(streams_of[1], (MEMBER_TALLY, DOMAIN_TILES, OMAX), 1.0, 6.0, ((0, 32), (1, 4)))
    measured_datum = noise(streams_of[2], (DOMAIN_TILES, OMAX), 2.0, 10.0, ((0, 128),), jnp.float32)
    weighted_inverse_noise = jnp.clip(jnp.exp(math.log(1.0) - 2.9996462 * jax.random.uniform(streams_of[3], (DOMAIN_TILES, OMAX), jnp.float32) ** level_of(streams_of[3], (DOMAIN_TILES, OMAX), ((0, 128),), -0.2, 0.2)), 0.049804688, 1.0).astype(jnp.bfloat16)
    local_tallies = draw_local_tallies(jax.random.fold_in(streams_of[6], 71), 0)
    device_assignment = draw_device_assignment(jax.random.fold_in(streams_of[6], 71), 0)
    return {"prior_trajectory": prior_trajectory, "measured_equivalent": measured_equivalent, "measured_datum": measured_datum, "weighted_inverse_noise": weighted_inverse_noise, "local_tallies": local_tallies, "device_assignment": device_assignment}


def solve_weights(cov, proj):
    size = cov.shape[-1]
    eye = jnp.eye(size, dtype=jnp.float32)
    amat = (size - 1.0) * eye + cov
    scale = jnp.sqrt(lax.optimization_barrier(jnp.sum(amat * amat, axis=(-2, -1), keepdims=True)))
    ymat = amat / scale
    zmat = jnp.zeros_like(amat) + eye
    high = lax.Precision.HIGHEST
    for _ in range(ITERS):
        tmat = 1.5 * eye - 0.5 * jnp.matmul(zmat, ymat, precision=high)
        ymat = jnp.matmul(ymat, tmat, precision=high)
        zmat = jnp.matmul(tmat, zmat, precision=high)
    root = zmat / jnp.sqrt(scale)
    inner = jnp.matmul(root, proj[..., None], precision=high)
    wmean = jnp.matmul(root, inner, precision=high)
    full = math.sqrt(size - 1.0) * root + wmean
    full = full + (1.0 - lax.optimization_barrier(jnp.sum(full, axis=-2, keepdims=True))) / size
    return full.astype(jnp.bfloat16)

def block_weights(ens_part, values, rinv, number):
    ybar = lax.optimization_barrier(jnp.mean(ens_part.astype(jnp.float32), axis=0))
    ypert = (ens_part.astype(jnp.float32) - ybar).astype(jnp.bfloat16)
    innov = (values - ybar).astype(jnp.bfloat16)
    slots = jnp.arange(values.shape[1], dtype=jnp.int32)
    live = slots[None, :] < number[:, None]
    rmask = jnp.where(live, rinv, jnp.zeros_like(rinv))
    scaled = ypert * rmask[None]
    cov = jnp.einsum('kjo,ljo->jkl', scaled.astype(jnp.float32), ypert.astype(jnp.float32))
    proj = jnp.einsum('kjo,jo->jk', scaled.astype(jnp.float32), innov.astype(jnp.float32))
    return solve_weights(cov, proj)

def reference(prior_trajectory, measured_equivalent, measured_datum, weighted_inverse_noise, local_tallies, device_assignment):
    realization_sequence, tile_sequence, vertical_sequence, dynamics_vector = prior_trajectory.shape
    tile_cohort = BLK_DEV
    ngroups = tile_sequence // tile_cohort

    def step(index, carry):
        result, stored = carry
        leading_displacement = (index * tile_cohort).astype(jnp.int32)
        quantity_sequence = lax.dynamic_slice_in_dim(prior_trajectory, leading_displacement, tile_cohort, 1)
        ens_part = lax.dynamic_slice_in_dim(measured_equivalent, leading_displacement, tile_cohort, 1)
        values = lax.dynamic_slice_in_dim(measured_datum, leading_displacement, tile_cohort, 0)
        rinv = lax.dynamic_slice_in_dim(weighted_inverse_noise, leading_displacement, tile_cohort, 0)
        number = lax.dynamic_slice_in_dim(local_tallies, leading_displacement, tile_cohort, 0)
        full = block_weights(ens_part, values, rinv, number)
        mixed = jnp.einsum('kjcv,jki->ijcv', quantity_sequence.astype(jnp.float32), full.astype(jnp.float32)).astype(jnp.bfloat16)
        result = lax.dynamic_update_slice_in_dim(result, mixed, leading_displacement, 1)
        stored = lax.dynamic_update_slice_in_dim(stored, full, leading_displacement, 0)
        return (result, stored)
    opening_outcome0 = jnp.zeros(prior_trajectory.shape, jnp.bfloat16)
    stored0 = jnp.zeros((tile_sequence, realization_sequence, realization_sequence), jnp.bfloat16)
    result, stored = lax.fori_loop(0, ngroups, step, (opening_outcome0, stored0))
    tab = device_assignment.reshape(N_GRP, N_MEM, BLK_DEV).transpose(1, 0, 2).reshape(N_MEM, N_GRP * BLK_DEV)
    onehot = (tab[..., None] == jnp.arange(N_GRP, dtype=jnp.int32)).astype(jnp.int32)
    before = jnp.cumsum(onehot, axis=1) - onehot
    rank = lax.optimization_barrier(jnp.sum(before * onehot, axis=-1))
    column = jnp.arange(N_MEM, dtype=jnp.int32)[:, None]
    slot = tab * (N_MEM * BLK_DEV) + column * BLK_DEV + rank
    slot_flat = slot.reshape(N_MEM, N_GRP, BLK_DEV).transpose(1, 0, 2).reshape(-1).astype(jnp.int32)
    order = jnp.argsort(slot_flat).astype(jnp.int32)
    slot_weights = jnp.take(stored, order, axis=0)
    return (result, slot_weights)
```

```python
import functools
import math

import jax
import jax.numpy as jnp
from jax import lax
from jax.experimental import pallas as pl
from jax.experimental.pallas import tpu as pltpu
from jax.sharding import PartitionSpec as P

ITERS = 12
MEM = 128
NBLK = 8
COLS = 8
VERT = 512
OBS = 1024
NGRP = 4
NMEM = 32
OWN = MEM // NMEM
CAP = NBLK // 2
ROWS = MEM * COLS
MESH = pl.DeviceIdType.MESH
HIGH = lax.Precision.HIGHEST
F32 = jnp.float32
BF16 = jnp.bfloat16


def mm(a, b):
    return jnp.dot(a, b, precision=HIGH, preferred_element_type=F32)


def analysis_kernel(
    prior, equiv, datum, winv, tally, table,
    out, slots,
    xg, yg, yf, kron, spread, ymat, zmat, pmat, scales, wts, pack, got, tabs, tab_mine,
    x_send, x_recv, y_send, y_recv, g_send, g_recv, t_send, t_recv, x_loc, y_loc,
):
    g = lax.axis_index("grp")
    m = lax.axis_index("mem")
    row, col, core = m // 8, (m // 2) % 4, m % 2

    def peer(i):
        return (((row + i // 8) % 4) * 4 + (col + (i // 2) % 4) % 4) * 2 + (core + i % 2) % 2

    barrier = pltpu.get_barrier_semaphore()

    def greet(i, carry):
        pl.semaphore_signal(barrier, inc=1, device_id=(g, peer(i)), device_id_type=MESH)
        return carry

    lax.fori_loop(1, NMEM, greet, 0)
    for d in range(1, NGRP):
        pl.semaphore_signal(barrier, inc=1, device_id=((g + d) % NGRP, m), device_id_type=MESH)
    pl.semaphore_wait(barrier, NMEM - 1 + NGRP - 1)

    def send_obs(i, carry):
        p = peer((i * 11) % NMEM)
        pltpu.make_async_remote_copy(
            src_ref=equiv.at[:, p], dst_ref=yg.at[pl.ds(OWN * m, OWN)],
            send_sem=y_send, recv_sem=y_recv, device_id=(g, p), device_id_type=MESH,
        ).start()
        return carry

    lax.fori_loop(1, NMEM, send_obs, 0)
    own_y = pltpu.make_async_copy(equiv.at[:, m], yg.at[pl.ds(OWN * m, OWN)], y_loc)
    own_y.start()

    def send_block(q, carry):
        def send_prior(i, inner):
            p = peer((i * 11) % NMEM)
            pltpu.make_async_remote_copy(
                src_ref=prior.at[:, pl.ds(NBLK * p + q, 1)],
                dst_ref=xg.at[pl.ds(OWN * m, OWN), pl.ds(q, 1)],
                send_sem=x_send, recv_sem=x_recv.at[q], device_id=(g, p), device_id_type=MESH,
            ).start()
            return inner

        return lax.fori_loop(1, NMEM, send_prior, carry)

    lax.fori_loop(0, NBLK, send_block, 0)
    own_x = pltpu.make_async_copy(
        prior.at[:, pl.ds(NBLK * m, NBLK)], xg.at[pl.ds(OWN * m, OWN)], x_loc)
    own_x.start()

    for j in range(NBLK):
        tab_mine[j:j + 1, :] = jnp.full((1, 128), table[j], jnp.int32)
    tab_copies = []
    for d in range(1, NGRP):
        c = pltpu.make_async_remote_copy(
            src_ref=tab_mine, dst_ref=tabs.at[g],
            send_sem=t_send.at[d], recv_sem=t_recv.at[d],
            device_id=((g + d) % NGRP, m), device_id_type=MESH)
        c.start()
        tab_copies.append(c)

    spread[...] = (
        lax.broadcasted_iota(jnp.int32, (MEM, ROWS), 0)
        == lax.broadcasted_iota(jnp.int32, (MEM, ROWS), 1) // COLS
    ).astype(F32).astype(BF16)
    eye = (
        lax.broadcasted_iota(jnp.int32, (MEM, MEM), 0)
        == lax.broadcasted_iota(jnp.int32, (MEM, MEM), 1)
    ).astype(F32)

    own_y.wait()
    landed = yg.at[pl.ds(0, MEM - OWN)]
    pltpu.make_async_copy(landed, landed, y_recv).wait()

    def add_member(k, acc):
        return acc + yg[k].astype(F32)

    total = lax.fori_loop(0, MEM, add_member, jnp.zeros((NBLK, OBS), F32))
    ybar = total * (1.0 / MEM)
    yf_mean = ybar

    def take_mean(k, carry):
        d = (yg[k].astype(F32) - yf_mean).astype(BF16).astype(F32)
        for ch in range(OBS // 128):
            yf[ch, pl.ds(pl.multiple_of(k * NBLK, NBLK), NBLK), :] = d[:, ch * 128:(ch + 1) * 128]
        return carry

    lax.fori_loop(0, MEM, take_mean, 0)
    innov = (datum[...] - ybar).astype(BF16).astype(F32)
    rinv = winv[...].astype(F32)
    for b in range(NBLK):
        live = lax.broadcasted_iota(jnp.int32, (1, OBS), 1) < tally[b]
        rmask = jnp.where(live, rinv[b:b + 1, :], 0.0)
        yp = jnp.concatenate(
            [yf[ch, pl.ds(b, MEM, stride=NBLK), :] for ch in range(OBS // 128)], axis=1)
        yr = (yp * rmask).astype(BF16)
        both = jnp.concatenate(
            [yp.astype(BF16), jnp.broadcast_to(innov[b:b + 1, :], (MEM, OBS)).astype(BF16)], axis=0)
        prod = lax.dot_general(yr, both, (((1,), (1,)), ((), ())), preferred_element_type=F32)
        amat = (MEM - 1.0) * eye + prod[:, :MEM]
        pmat[b] = prod[:, MEM:]
        scale = jnp.sqrt(jnp.sum(jnp.sum(amat * amat, axis=1, keepdims=True), axis=0, keepdims=True))
        scales[b] = jnp.broadcast_to(scale, (8, 128))
        ymat[b] = amat / scale
        zmat[b] = eye

    def newton(it, carry):
        ts = [1.5 * eye - 0.5 * mm(zmat[b], ymat[b]) for b in range(NBLK)]
        for b in range(NBLK):
            ymat[b] = mm(ymat[b], ts[b])
            zmat[b] = mm(ts[b], zmat[b])
        return carry

    lax.fori_loop(0, ITERS, newton, 0)

    for b in range(NBLK):
        root = zmat[b] / jnp.sqrt(scales[b][:1])
        wmean = mm(root, mm(root, pmat[b]))
        full = math.sqrt(MEM - 1.0) * root + wmean
        full = full + (1.0 - jnp.sum(full, axis=0, keepdims=True)) / MEM
        wts[b] = full.astype(BF16)

    within = []
    for j in range(NBLK):
        n = jnp.int32(0)
        for k in range(j):
            n = n + (table[k] == table[j]).astype(jnp.int32)
        within.append(n)
    for t in range(NGRP):
        for w in range(CAP):
            src = jnp.int32(0)
            for j in range(NBLK):
                src = src + jnp.int32(j) * ((table[j] == t) & (within[j] == w)).astype(jnp.int32)
            pack[t, w] = wts[src]
    w_copies = []
    for d in range(1, NGRP):
        to = (g + d) % NGRP
        c = pltpu.make_async_remote_copy(
            src_ref=pack.at[to], dst_ref=got.at[g],
            send_sem=g_send.at[d], recv_sem=g_recv.at[d],
            device_id=(to, m), device_id_type=MESH)
        c.start()
        w_copies.append(c)

    mask = (
        lax.broadcasted_iota(jnp.int32, (COLS, ROWS), 0)
        == lax.broadcasted_iota(jnp.int32, (COLS, ROWS), 1) % COLS
    ).astype(F32)

    def expand(b, carry):
        wide = lax.dot_general(
            wts[b], spread[...], (((0,), (0,)), ((), ())), preferred_element_type=F32)
        kron[b] = (wide[:, None, :] * mask[None]).reshape(ROWS, ROWS).astype(BF16)
        return carry

    lax.fori_loop(0, NBLK, expand, 0)

    for c in tab_copies:
        c.wait()
    for c in w_copies:
        c.wait()
    tabs[g] = tab_mine[...]
    got[g] = pack[g]
    base = jnp.zeros((1, 128), jnp.int32)
    ranks = []
    for gg in range(NGRP):
        hits = tabs[gg] == g
        count = jnp.sum(hits.astype(F32), axis=0, keepdims=True).astype(jnp.int32)
        for w in range(CAP):
            ranks.append(jnp.where(count > w, base + w, -1))
        base = base + count
    for k in range(NBLK):
        acc = jnp.zeros((MEM, MEM), F32)
        for gg in range(NGRP):
            for w in range(CAP):
                acc = jnp.where(ranks[gg * CAP + w] == k, got[gg, w].astype(F32), acc)
        slots[k] = acc.astype(BF16)

    own_x.wait()
    step = MEM // 4

    def mix(q, carry):
        here = xg.at[pl.ds(0, MEM - OWN), pl.ds(q, 1)]
        pltpu.make_async_copy(here, here, x_recv.at[q]).wait()
        state = xg[:, q].astype(F32).reshape(ROWS, VERT).astype(BF16)
        for part in range(4):
            mixed = jnp.dot(
                kron[q, part * step * COLS:(part + 1) * step * COLS, :], state,
                preferred_element_type=F32)
            out[part * step:(part + 1) * step, q] = mixed.reshape(step, COLS, VERT).astype(BF16)
        return carry

    lax.fori_loop(0, NBLK, mix, 0)

    sent = yg.at[pl.ds(0, MEM - OWN)]
    pltpu.make_async_copy(sent, sent, y_send).wait()
    sent = xg.at[pl.ds(0, MEM - OWN)]
    pltpu.make_async_copy(sent, sent, x_send).wait()


def store_kernel(analysis, slots, out, out_slots, sems):
    part = MEM // 8
    copies = [
        pltpu.make_async_copy(analysis.at[pl.ds(k * part, part)], out.at[pl.ds(k * part, part)], sems.at[k])
        for k in range(8)
    ]
    copies.append(pltpu.make_async_copy(slots, out_slots, sems.at[8]))
    for c in copies:
        c.start()
    for c in copies:
        c.wait()


def body(prior, equiv, datum, winv, tally, table):
    vmem = pl.BlockSpec(memory_space=pltpu.VMEM)
    smem = pl.BlockSpec(memory_space=pltpu.SMEM)
    hbm = pl.BlockSpec(memory_space=pltpu.HBM)
    dma = pltpu.SemaphoreType.DMA
    equiv = equiv.reshape(OWN, NMEM, NBLK, OBS)
    analysis, slots = pl.pallas_call(
        analysis_kernel,
        out_shape=(
            pltpu.VMEM((MEM, NBLK, COLS, VERT), BF16),
            pltpu.VMEM((NBLK, MEM, MEM), BF16),
        ),
        in_specs=[hbm, hbm, vmem, vmem, smem, smem],
        out_specs=(vmem, vmem),
        scratch_shapes=[
            pltpu.VMEM((MEM, NBLK, COLS, VERT), BF16),
            pltpu.VMEM((MEM, NBLK, OBS), BF16),
            pltpu.VMEM((OBS // 128, MEM * NBLK, 128), F32),
            pltpu.VMEM((NBLK, ROWS, ROWS), BF16),
            pltpu.VMEM((MEM, ROWS), BF16),
            pltpu.VMEM((NBLK, MEM, MEM), F32),
            pltpu.VMEM((NBLK, MEM, MEM), F32),
            pltpu.VMEM((NBLK, MEM, MEM), F32),
            pltpu.VMEM((NBLK, 8, 128), F32),
            pltpu.VMEM((NBLK, MEM, MEM), BF16),
            pltpu.VMEM((NGRP, CAP, MEM, MEM), BF16),
            pltpu.VMEM((NGRP, CAP, MEM, MEM), BF16),
            pltpu.VMEM((NGRP, NBLK, 128), jnp.int32),
            pltpu.VMEM((NBLK, 128), jnp.int32),
            dma, dma((NBLK,)), dma, dma,
            dma((NGRP,)), dma((NGRP,)), dma((NGRP,)), dma((NGRP,)), dma, dma,
        ],
        compiler_params=pltpu.CompilerParams(
            collective_id=0, has_side_effects=True, vmem_limit_bytes=50 << 20),
        name="analyse",
    )(prior, equiv, datum, winv, tally, table)
    return pl.pallas_call(
        store_kernel,
        out_shape=(
            jax.ShapeDtypeStruct((MEM, NBLK, COLS, VERT), BF16),
            jax.ShapeDtypeStruct((NBLK, MEM, MEM), BF16),
        ),
        in_specs=[vmem, vmem],
        out_specs=(hbm, hbm),
        scratch_shapes=[dma((9,))],
        compiler_params=pltpu.CompilerParams(vmem_limit_bytes=40 << 20),
        name="store",
    )(analysis, slots)


def solution(mesh):
    return jax.shard_map(
        body,
        mesh=mesh,
        in_specs=(
            P("mem", "grp", None, None),
            P("mem", "grp", None),
            P(("grp", "mem"), None),
            P(("grp", "mem"), None),
            P(("grp", "mem")),
            P(("grp", "mem")),
        ),
        out_specs=(P(None, ("grp", "mem"), None, None), P(("grp", "mem"), None, None)),
        check_vma=False,
    )
```

```python
import functools
import math

import jax
import jax.numpy as jnp
from jax import lax
from jax.experimental import pallas as pl
from jax.experimental.pallas import tpu as pltpu
from jax.sharding import PartitionSpec as P

ITERS = 12
MEM = 128
NBLK = 8
COLS = 8
VERT = 512
OBS = 1024
NGRP = 4
NMEM = 32
OWN = MEM // NMEM
CAP = NBLK // 2
LAST = NBLK - 1
HALF = OWN // 2
PARTS = 4
STEP = MEM // PARTS
ROWS = MEM * COLS
MESH = pl.DeviceIdType.MESH
HIGH = lax.Precision.HIGHEST
F32 = jnp.float32
BF16 = jnp.bfloat16


def mm(a, b):
    return jnp.dot(a, b, precision=HIGH, preferred_element_type=F32)


def analysis_kernel(
    prior, equiv, datum_hbm, winv_hbm, tally_hbm, table_hbm,
    out, slots, xlast, klast,
    xg, yg, datum, winv, tally, table, yf, kron, spread, ymat, zmat, pmat, scales, wts, pack, got, tabs, tab_mine,
    x_send, x_recv, y_send, y_recv, g_send, g_recv, t_send, t_recv, x_loc, y_loc, s_loc,
):
    g = lax.axis_index("grp")
    m = lax.axis_index("mem")
    row, col, core = m // 8, (m // 2) % 4, m % 2

    def peer(i):
        return (((row + i // 8) % 4) * 4 + (col + (i // 2) % 4) % 4) * 2 + (core + i % 2) % 2

    barrier = pltpu.get_barrier_semaphore()

    def greet(i, carry):
        pl.semaphore_signal(barrier, inc=1, device_id=(g, peer(i)), device_id_type=MESH)
        return carry

    lax.fori_loop(1, NMEM, greet, 0)
    for d in range(1, NGRP):
        pl.semaphore_signal(barrier, inc=1, device_id=((g + d) % NGRP, m), device_id_type=MESH)
    pl.semaphore_wait(barrier, NMEM - 1 + NGRP - 1)

    def send_obs(i, carry):
        p = peer((i % (NMEM - 1) + 1) * 5 % NMEM)
        part = i // (NMEM - 1)
        pltpu.make_async_remote_copy(
            src_ref=equiv.at[pl.ds(part, 1), p], dst_ref=yg.at[pl.ds(OWN * m + part, 1)],
            send_sem=y_send, recv_sem=y_recv, device_id=(g, p), device_id_type=MESH,
        ).start()
        return carry

    lax.fori_loop(0, OWN * (NMEM - 1), send_obs, 0)
    own_y = pltpu.make_async_copy(equiv.at[:, m], yg.at[pl.ds(OWN * m, OWN)], y_loc)
    own_y.start()

    small = [
        pltpu.make_async_copy(a, b, s_loc.at[n])
        for n, (a, b) in enumerate(
            ((datum_hbm, datum), (winv_hbm, winv), (tally_hbm, tally), (table_hbm, table)))
    ]
    for c in small:
        c.start()

    def send_block(q, land, sem):
        def send_prior(i, inner):
            p = peer((i % (NMEM - 1) + 1) * 5 % NMEM)
            part = HALF * (i // (NMEM - 1))
            pltpu.make_async_remote_copy(
                src_ref=prior.at[pl.ds(part, HALF), pl.ds(NBLK * p + q, 1)],
                dst_ref=land(pl.ds(OWN * m + part, HALF)),
                send_sem=sem, recv_sem=x_recv.at[q], device_id=(g, p), device_id_type=MESH,
            ).start()
            return inner

        return lax.fori_loop(0, OWN // HALF * (NMEM - 1), send_prior, 0)

    def send_early(q, carry):
        send_block(q, lambda rows: xg.at[rows, pl.ds(q, 1)], x_send.at[0])
        return carry

    lax.fori_loop(0, LAST, send_early, 0)
    send_block(LAST, lambda rows: xlast.at[rows], x_send.at[1])
    own_x = [
        pltpu.make_async_copy(
            prior.at[:, pl.ds(NBLK * m, LAST)], xg.at[pl.ds(OWN * m, OWN)], x_loc.at[0]),
        pltpu.make_async_copy(
            prior.at[:, pl.ds(NBLK * m + LAST, 1)], xlast.at[pl.ds(OWN * m, OWN)], x_loc.at[1]),
    ]
    for c in own_x:
        c.start()

    for c in small:
        c.wait()

    for j in range(NBLK):
        tab_mine[j:j + 1, :] = jnp.full((1, 128), table[j], jnp.int32)
    tab_copies = []
    for d in range(1, NGRP):
        c = pltpu.make_async_remote_copy(
            src_ref=tab_mine, dst_ref=tabs.at[g],
            send_sem=t_send.at[d], recv_sem=t_recv.at[d],
            device_id=((g + d) % NGRP, m), device_id_type=MESH)
        c.start()
        tab_copies.append(c)

    spread[...] = (
        lax.broadcasted_iota(jnp.int32, (MEM, ROWS), 0)
        == lax.broadcasted_iota(jnp.int32, (MEM, ROWS), 1) // COLS
    ).astype(F32).astype(BF16)
    eye = (
        lax.broadcasted_iota(jnp.int32, (MEM, MEM), 0)
        == lax.broadcasted_iota(jnp.int32, (MEM, MEM), 1)
    ).astype(F32)

    own_y.wait()
    landed = yg.at[pl.ds(0, MEM - OWN)]
    pltpu.make_async_copy(landed, landed, y_recv).wait()

    def add_member(k, acc):
        return acc + yg[k].astype(F32)

    total = lax.fori_loop(0, MEM, add_member, jnp.zeros((NBLK, OBS), F32))
    ybar = total * (1.0 / MEM)
    yf_mean = ybar

    def take_mean(k, carry):
        d = (yg[k].astype(F32) - yf_mean).astype(BF16).astype(F32)
        for ch in range(OBS // 128):
            yf[ch, pl.ds(pl.multiple_of(k * NBLK, NBLK), NBLK), :] = d[:, ch * 128:(ch + 1) * 128]
        return carry

    lax.fori_loop(0, MEM, take_mean, 0)
    innov = (datum[...] - ybar).astype(BF16).astype(F32)
    rinv = winv[...].astype(F32)
    for b in range(NBLK):
        live = lax.broadcasted_iota(jnp.int32, (1, OBS), 1) < tally[b]
        rmask = jnp.where(live, rinv[b:b + 1, :], 0.0)
        yp = jnp.concatenate(
            [yf[ch, pl.ds(b, MEM, stride=NBLK), :] for ch in range(OBS // 128)], axis=1)
        yr = (yp * rmask).astype(BF16)
        both = jnp.concatenate(
            [yp.astype(BF16), jnp.broadcast_to(innov[b:b + 1, :], (MEM, OBS)).astype(BF16)], axis=0)
        prod = lax.dot_general(yr, both, (((1,), (1,)), ((), ())), preferred_element_type=F32)
        amat = (MEM - 1.0) * eye + prod[:, :MEM]
        pmat[b] = prod[:, MEM:]
        scale = jnp.sqrt(jnp.sum(jnp.sum(amat * amat, axis=1, keepdims=True), axis=0, keepdims=True))
        scales[b] = jnp.broadcast_to(scale, (8, 128))
        ymat[b] = amat / scale
        zmat[b] = eye

    def newton(it, carry):
        ts = [1.5 * eye - 0.5 * mm(zmat[b], ymat[b]) for b in range(NBLK)]
        for b in range(NBLK):
            ymat[b] = mm(ymat[b], ts[b])
            zmat[b] = mm(ts[b], zmat[b])
        return carry

    lax.fori_loop(0, ITERS, newton, 0)

    for b in range(NBLK):
        root = zmat[b] / jnp.sqrt(scales[b][:1])
        wmean = mm(root, mm(root, pmat[b]))
        full = math.sqrt(MEM - 1.0) * root + wmean
        full = full + (1.0 - jnp.sum(full, axis=0, keepdims=True)) / MEM
        wts[b] = full.astype(BF16)

    within = []
    for j in range(NBLK):
        n = jnp.int32(0)
        for k in range(j):
            n = n + (table[k] == table[j]).astype(jnp.int32)
        within.append(n)
    for t in range(NGRP):
        for w in range(CAP):
            src = jnp.int32(0)
            for j in range(NBLK):
                src = src + jnp.int32(j) * ((table[j] == t) & (within[j] == w)).astype(jnp.int32)
            pack[t, w] = wts[src]
    w_copies = []
    for d in range(1, NGRP):
        to = (g + d) % NGRP
        c = pltpu.make_async_remote_copy(
            src_ref=pack.at[to], dst_ref=got.at[g],
            send_sem=g_send.at[d], recv_sem=g_recv.at[d],
            device_id=(to, m), device_id_type=MESH)
        c.start()
        w_copies.append(c)

    mask = (
        lax.broadcasted_iota(jnp.int32, (COLS, ROWS), 0)
        == lax.broadcasted_iota(jnp.int32, (COLS, ROWS), 1) % COLS
    ).astype(F32)

    def expanded(b):
        wide = lax.dot_general(
            wts[b], spread[...], (((0,), (0,)), ((), ())), preferred_element_type=F32)
        return (wide[:, None, :] * mask[None]).reshape(ROWS, ROWS).astype(BF16)

    def expand(b, carry):
        kron[b] = expanded(b)
        return carry

    lax.fori_loop(0, LAST, expand, 0)
    klast[...] = expanded(LAST)

    for c in tab_copies:
        c.wait()
    for c in w_copies:
        c.wait()
    tabs[g] = tab_mine[...]
    got[g] = pack[g]
    base = jnp.zeros((1, 128), jnp.int32)
    ranks = []
    for gg in range(NGRP):
        hits = tabs[gg] == g
        count = jnp.sum(hits.astype(F32), axis=0, keepdims=True).astype(jnp.int32)
        for w in range(CAP):
            ranks.append(jnp.where(count > w, base + w, -1))
        base = base + count
    for k in range(NBLK):
        acc = jnp.zeros((MEM, MEM), F32)
        for gg in range(NGRP):
            for w in range(CAP):
                acc = jnp.where(ranks[gg * CAP + w] == k, got[gg, w].astype(F32), acc)
        slots[k] = acc.astype(BF16)

    for c in own_x:
        c.wait()

    def mix(q, carry):
        here = xg.at[pl.ds(0, MEM - OWN), pl.ds(q, 1)]
        pltpu.make_async_copy(here, here, x_recv.at[q]).wait()
        state = xg[:, q].astype(F32).reshape(ROWS, VERT).astype(BF16)
        for part in range(PARTS):
            out[part * STEP:(part + 1) * STEP, q] = mixed(kron.at[q], state, part)
        return carry

    lax.fori_loop(0, LAST, mix, 0)
    here = xlast.at[pl.ds(0, MEM - OWN)]
    pltpu.make_async_copy(here, here, x_recv.at[LAST]).wait()

    sent = yg.at[pl.ds(0, MEM - OWN)]
    pltpu.make_async_copy(sent, sent, y_send).wait()
    sent = xg.at[pl.ds(0, MEM - OWN)]
    pltpu.make_async_copy(sent, sent, x_send.at[0]).wait()
    sent = xlast.at[pl.ds(0, MEM - OWN)]
    pltpu.make_async_copy(sent, sent, x_send.at[1]).wait()


def mixed(weights, state, part):
    rows = weights[part * STEP * COLS:(part + 1) * STEP * COLS, :]
    total = jnp.dot(rows, state, preferred_element_type=F32)
    return total.reshape(STEP, COLS, VERT).astype(BF16)


def store_kernel(analysis, slots, xlast, klast, out, out_slots, made, sems):
    copies = [
        pltpu.make_async_copy(analysis, out.at[:, pl.ds(0, LAST)], sems.at[PARTS]),
        pltpu.make_async_copy(slots, out_slots, sems.at[PARTS + 1]),
    ]
    for c in copies:
        c.start()
    state = xlast[:, 0].astype(F32).reshape(ROWS, VERT).astype(BF16)
    for part in range(PARTS):
        rows = pl.ds(part * STEP, STEP)
        made[rows, 0] = mixed(klast, state, part)
        c = pltpu.make_async_copy(made.at[rows], out.at[rows, pl.ds(LAST, 1)], sems.at[part])
        c.start()
        copies.append(c)
    for c in copies:
        c.wait()


def body(prior, equiv, datum, winv, tally, table):
    vmem = pl.BlockSpec(memory_space=pltpu.VMEM)
    hbm = pl.BlockSpec(memory_space=pltpu.HBM)
    dma = pltpu.SemaphoreType.DMA
    equiv = equiv.reshape(OWN, NMEM, NBLK, OBS)
    made = pl.pallas_call(
        analysis_kernel,
        out_shape=(
            pltpu.VMEM((MEM, LAST, COLS, VERT), BF16),
            pltpu.VMEM((NBLK, MEM, MEM), BF16),
            pltpu.VMEM((MEM, 1, COLS, VERT), BF16),
            pltpu.VMEM((ROWS, ROWS), BF16),
        ),
        in_specs=[hbm] * 6,
        out_specs=(vmem,) * 4,
        scratch_shapes=[
            pltpu.VMEM((MEM, LAST, COLS, VERT), BF16),
            pltpu.VMEM((MEM, NBLK, OBS), BF16),
            pltpu.VMEM((NBLK, OBS), F32),
            pltpu.VMEM((NBLK, OBS), BF16),
            pltpu.SMEM((NBLK,), jnp.int32),
            pltpu.SMEM((NBLK,), jnp.int32),
            pltpu.VMEM((OBS // 128, MEM * NBLK, 128), F32),
            pltpu.VMEM((LAST, ROWS, ROWS), BF16),
            pltpu.VMEM((MEM, ROWS), BF16),
            pltpu.VMEM((NBLK, MEM, MEM), F32),
            pltpu.VMEM((NBLK, MEM, MEM), F32),
            pltpu.VMEM((NBLK, MEM, MEM), F32),
            pltpu.VMEM((NBLK, 8, 128), F32),
            pltpu.VMEM((NBLK, MEM, MEM), BF16),
            pltpu.VMEM((NGRP, CAP, MEM, MEM), BF16),
            pltpu.VMEM((NGRP, CAP, MEM, MEM), BF16),
            pltpu.VMEM((NGRP, NBLK, 128), jnp.int32),
            pltpu.VMEM((NBLK, 128), jnp.int32),
            dma((2,)), dma((NBLK,)), dma, dma,
            dma((NGRP,)), dma((NGRP,)), dma((NGRP,)), dma((NGRP,)), dma((2,)), dma, dma((4,)),
        ],
        compiler_params=pltpu.CompilerParams(
            collective_id=0, has_side_effects=True, vmem_limit_bytes=46 << 20),
        name="analyse",
    )(prior, equiv, datum, winv, tally, table)
    return pl.pallas_call(
        store_kernel,
        out_shape=(
            jax.ShapeDtypeStruct((MEM, NBLK, COLS, VERT), BF16),
            jax.ShapeDtypeStruct((NBLK, MEM, MEM), BF16),
        ),
        in_specs=[vmem] * 4,
        out_specs=(hbm, hbm),
        scratch_shapes=[pltpu.VMEM((MEM, 1, COLS, VERT), BF16), dma((PARTS + 2,))],
        compiler_params=pltpu.CompilerParams(vmem_limit_bytes=40 << 20),
        name="store",
    )(*made)


def solution(mesh):
    return jax.shard_map(
        body,
        mesh=mesh,
        in_specs=(
            P("mem", "grp", None, None),
            P("mem", "grp", None),
            P(("grp", "mem"), None),
            P(("grp", "mem"), None),
            P(("grp", "mem")),
            P(("grp", "mem")),
        ),
        out_specs=(P(None, ("grp", "mem"), None, None), P(("grp", "mem"), None, None)),
        check_vma=False,
    )
```

```python
import functools
import math

import jax
import jax.numpy as jnp
from jax import lax
from jax.experimental import pallas as pl
from jax.experimental.pallas import tpu as pltpu
from jax.sharding import PartitionSpec as P

ITERS = 12
MEM = 128
NBLK = 8
COLS = 8
VERT = 512
OBS = 1024
NGRP = 4
NMEM = 32
OWN = MEM // NMEM
CAP = NBLK // 2
LAST = NBLK - 1
HALF = OWN // 2
PARTS = 4
STEP = MEM // PARTS
ROWS = MEM * COLS
MESH = pl.DeviceIdType.MESH
HIGH = lax.Precision.HIGHEST
F32 = jnp.float32
BF16 = jnp.bfloat16


def mm(a, b):
    return jnp.dot(a, b, precision=HIGH, preferred_element_type=F32)


def analysis_kernel(
    prior, equiv, datum_hbm, winv_hbm, tally_hbm, table_hbm,
    out, slots, xlast, klast,
    xg, yg, datum, winv, tally, table, yf, kron, spread, ymat, zmat, pmat, scales, wts, pack, got, tabs, tab_mine,
    x_send, x_recv, y_send, y_recv, g_send, g_recv, t_send, t_recv, x_loc, y_loc, s_loc,
):
    g = lax.axis_index("grp")
    m = lax.axis_index("mem")
    row, col, core = m // 8, (m // 2) % 4, m % 2

    def peer(i):
        return (((row + i // 8) % 4) * 4 + (col + (i // 2) % 4) % 4) * 2 + (core + i % 2) % 2

    barrier = pltpu.get_barrier_semaphore()

    def greet(i, carry):
        pl.semaphore_signal(barrier, inc=1, device_id=(g, peer(i)), device_id_type=MESH)
        return carry

    lax.fori_loop(1, NMEM, greet, 0)
    for d in range(1, NGRP):
        pl.semaphore_signal(barrier, inc=1, device_id=((g + d) % NGRP, m), device_id_type=MESH)
    pl.semaphore_wait(barrier, NMEM - 1 + NGRP - 1)

    def send_obs(i, carry):
        p = peer((i % (NMEM - 1) + 1) * 5 % NMEM)
        part = i // (NMEM - 1)
        pltpu.make_async_remote_copy(
            src_ref=equiv.at[pl.ds(part, 1), p], dst_ref=yg.at[pl.ds(OWN * m + part, 1)],
            send_sem=y_send, recv_sem=y_recv, device_id=(g, p), device_id_type=MESH,
        ).start()
        return carry

    lax.fori_loop(0, OWN * (NMEM - 1), send_obs, 0)
    own_y = pltpu.make_async_copy(equiv.at[:, m], yg.at[pl.ds(OWN * m, OWN)], y_loc)
    own_y.start()

    small = [
        pltpu.make_async_copy(a, b, s_loc.at[n])
        for n, (a, b) in enumerate(
            ((datum_hbm, datum), (winv_hbm, winv), (tally_hbm, tally), (table_hbm, table)))
    ]
    for c in small:
        c.start()

    def send_block(q, land, sem):
        def send_prior(i, inner):
            p = peer((i % (NMEM - 1) + 1) * 5 % NMEM)
            part = HALF * (i // (NMEM - 1))
            pltpu.make_async_remote_copy(
                src_ref=prior.at[pl.ds(part, HALF), pl.ds(NBLK * p + q, 1)],
                dst_ref=land(pl.ds(OWN * m + part, HALF)),
                send_sem=sem, recv_sem=x_recv.at[q], device_id=(g, p), device_id_type=MESH,
            ).start()
            return inner

        return lax.fori_loop(0, OWN // HALF * (NMEM - 1), send_prior, 0)

    def send_early(q, carry):
        send_block(q, lambda rows: xg.at[rows, pl.ds(q, 1)], x_send.at[0])
        return carry

    lax.fori_loop(0, LAST, send_early, 0)
    far = sorted(range(1, NMEM), key=lambda i: -(min(i // 8, 4 - i // 8) + min((i // 2) % 4, 4 - (i // 2) % 4)))
    for i in far:
        for part in range(0, OWN, HALF):
            p = peer(i)
            pltpu.make_async_remote_copy(
                src_ref=prior.at[pl.ds(part, HALF), pl.ds(NBLK * p + LAST, 1)],
                dst_ref=xlast.at[pl.ds(OWN * m + part, HALF)],
                send_sem=x_send.at[1], recv_sem=x_recv.at[LAST], device_id=(g, p), device_id_type=MESH,
            ).start()
    own_x = [
        pltpu.make_async_copy(
            prior.at[:, pl.ds(NBLK * m, LAST)], xg.at[pl.ds(OWN * m, OWN)], x_loc.at[0]),
        pltpu.make_async_copy(
            prior.at[:, pl.ds(NBLK * m + LAST, 1)], xlast.at[pl.ds(OWN * m, OWN)], x_loc.at[1]),
    ]
    for c in own_x:
        c.start()

    for c in small:
        c.wait()

    for j in range(NBLK):
        tab_mine[j:j + 1, :] = jnp.full((1, 128), table[j], jnp.int32)
    tab_copies = []
    for d in range(1, NGRP):
        c = pltpu.make_async_remote_copy(
            src_ref=tab_mine, dst_ref=tabs.at[g],
            send_sem=t_send.at[d], recv_sem=t_recv.at[d],
            device_id=((g + d) % NGRP, m), device_id_type=MESH)
        c.start()
        tab_copies.append(c)

    spread[...] = (
        lax.broadcasted_iota(jnp.int32, (MEM, ROWS), 0)
        == lax.broadcasted_iota(jnp.int32, (MEM, ROWS), 1) // COLS
    ).astype(F32).astype(BF16)
    eye = (
        lax.broadcasted_iota(jnp.int32, (MEM, MEM), 0)
        == lax.broadcasted_iota(jnp.int32, (MEM, MEM), 1)
    ).astype(F32)

    own_y.wait()
    landed = yg.at[pl.ds(0, MEM - OWN)]
    pltpu.make_async_copy(landed, landed, y_recv).wait()

    def add_member(k, acc):
        return acc + yg[k].astype(F32)

    total = lax.fori_loop(0, MEM, add_member, jnp.zeros((NBLK, OBS), F32))
    ybar = total * (1.0 / MEM)
    yf_mean = ybar

    def take_mean(k, carry):
        d = (yg[k].astype(F32) - yf_mean).astype(BF16).astype(F32)
        for ch in range(OBS // 128):
            yf[ch, pl.ds(pl.multiple_of(k * NBLK, NBLK), NBLK), :] = d[:, ch * 128:(ch + 1) * 128]
        return carry

    lax.fori_loop(0, MEM, take_mean, 0)
    innov = (datum[...] - ybar).astype(BF16).astype(F32)
    rinv = winv[...].astype(F32)
    for b in range(NBLK):
        live = lax.broadcasted_iota(jnp.int32, (1, OBS), 1) < tally[b]
        rmask = jnp.where(live, rinv[b:b + 1, :], 0.0)
        yp = jnp.concatenate(
            [yf[ch, pl.ds(b, MEM, stride=NBLK), :] for ch in range(OBS // 128)], axis=1)
        yr = (yp * rmask).astype(BF16)
        both = jnp.concatenate(
            [yp.astype(BF16), jnp.broadcast_to(innov[b:b + 1, :], (MEM, OBS)).astype(BF16)], axis=0)
        prod = lax.dot_general(yr, both, (((1,), (1,)), ((), ())), preferred_element_type=F32)
        amat = (MEM - 1.0) * eye + prod[:, :MEM]
        pmat[b] = prod[:, MEM:]
        scale = jnp.sqrt(jnp.sum(jnp.sum(amat * amat, axis=1, keepdims=True), axis=0, keepdims=True))
        scales[b] = jnp.broadcast_to(scale, (8, 128))
        ymat[b] = amat / scale
        zmat[b] = eye

    def newton(it, carry):
        ts = [1.5 * eye - 0.5 * mm(zmat[b], ymat[b]) for b in range(NBLK)]
        for b in range(NBLK):
            ymat[b] = mm(ymat[b], ts[b])
            zmat[b] = mm(ts[b], zmat[b])
        return carry

    lax.fori_loop(0, ITERS, newton, 0)

    for b in range(NBLK):
        root = zmat[b] / jnp.sqrt(scales[b][:1])
        wmean = mm(root, mm(root, pmat[b]))
        full = math.sqrt(MEM - 1.0) * root + wmean
        full = full + (1.0 - jnp.sum(full, axis=0, keepdims=True)) / MEM
        wts[b] = full.astype(BF16)

    within = []
    for j in range(NBLK):
        n = jnp.int32(0)
        for k in range(j):
            n = n + (table[k] == table[j]).astype(jnp.int32)
        within.append(n)
    for t in range(NGRP):
        for w in range(CAP):
            src = jnp.int32(0)
            for j in range(NBLK):
                src = src + jnp.int32(j) * ((table[j] == t) & (within[j] == w)).astype(jnp.int32)
            pack[t, w] = wts[src]
    w_copies = []
    for d in range(1, NGRP):
        to = (g + d) % NGRP
        c = pltpu.make_async_remote_copy(
            src_ref=pack.at[to], dst_ref=got.at[g],
            send_sem=g_send.at[d], recv_sem=g_recv.at[d],
            device_id=(to, m), device_id_type=MESH)
        c.start()
        w_copies.append(c)

    mask = (
        lax.broadcasted_iota(jnp.int32, (COLS, ROWS), 0)
        == lax.broadcasted_iota(jnp.int32, (COLS, ROWS), 1) % COLS
    ).astype(F32)

    def expanded(b):
        wide = lax.dot_general(
            wts[b], spread[...], (((0,), (0,)), ((), ())), preferred_element_type=F32)
        return (wide[:, None, :] * mask[None]).reshape(ROWS, ROWS).astype(BF16)

    def expand(b, carry):
        kron[b] = expanded(b)
        return carry

    lax.fori_loop(0, LAST, expand, 0)
    klast[...] = expanded(LAST)

    for c in tab_copies:
        c.wait()
    for c in w_copies:
        c.wait()
    tabs[g] = tab_mine[...]
    got[g] = pack[g]
    base = jnp.zeros((1, 128), jnp.int32)
    ranks = []
    for gg in range(NGRP):
        hits = tabs[gg] == g
        count = jnp.sum(hits.astype(F32), axis=0, keepdims=True).astype(jnp.int32)
        for w in range(CAP):
            ranks.append(jnp.where(count > w, base + w, -1))
        base = base + count
    for k in range(NBLK):
        acc = jnp.zeros((MEM, MEM), F32)
        for gg in range(NGRP):
            for w in range(CAP):
                acc = jnp.where(ranks[gg * CAP + w] == k, got[gg, w].astype(F32), acc)
        slots[k] = acc.astype(BF16)

    for c in own_x:
        c.wait()

    def mix(q, carry):
        here = xg.at[pl.ds(0, MEM - OWN), pl.ds(q, 1)]
        pltpu.make_async_copy(here, here, x_recv.at[q]).wait()
        state = xg[:, q].astype(F32).reshape(ROWS, VERT).astype(BF16)
        for part in range(PARTS):
            out[part * STEP:(part + 1) * STEP, q] = mixed(kron.at[q], state, part)
        return carry

    lax.fori_loop(0, LAST, mix, 0)
    here = xlast.at[pl.ds(0, MEM - OWN)]
    pltpu.make_async_copy(here, here, x_recv.at[LAST]).wait()

    sent = yg.at[pl.ds(0, MEM - OWN)]
    pltpu.make_async_copy(sent, sent, y_send).wait()
    sent = xg.at[pl.ds(0, MEM - OWN)]
    pltpu.make_async_copy(sent, sent, x_send.at[0]).wait()
    sent = xlast.at[pl.ds(0, MEM - OWN)]
    pltpu.make_async_copy(sent, sent, x_send.at[1]).wait()


def mixed(weights, state, part):
    rows = weights[part * STEP * COLS:(part + 1) * STEP * COLS, :]
    total = jnp.dot(rows, state, preferred_element_type=F32)
    return total.reshape(STEP, COLS, VERT).astype(BF16)


def store_kernel(analysis, slots, xlast, klast, out, out_slots, made, sems):
    copies = [
        pltpu.make_async_copy(analysis, out.at[:, pl.ds(0, LAST)], sems.at[PARTS]),
        pltpu.make_async_copy(slots, out_slots, sems.at[PARTS + 1]),
    ]
    for c in copies:
        c.start()
    state = xlast[:, 0].astype(F32).reshape(ROWS, VERT).astype(BF16)
    for part in range(PARTS):
        rows = pl.ds(part * STEP, STEP)
        made[rows, 0] = mixed(klast, state, part)
        c = pltpu.make_async_copy(made.at[rows], out.at[rows, pl.ds(LAST, 1)], sems.at[part])
        c.start()
        copies.append(c)
    for c in copies:
        c.wait()


def body(prior, equiv, datum, winv, tally, table):
    vmem = pl.BlockSpec(memory_space=pltpu.VMEM)
    hbm = pl.BlockSpec(memory_space=pltpu.HBM)
    dma = pltpu.SemaphoreType.DMA
    equiv = equiv.reshape(OWN, NMEM, NBLK, OBS)
    made = pl.pallas_call(
        analysis_kernel,
        out_shape=(
            pltpu.VMEM((MEM, LAST, COLS, VERT), BF16),
            pltpu.VMEM((NBLK, MEM, MEM), BF16),
            pltpu.VMEM((MEM, 1, COLS, VERT), BF16),
            pltpu.VMEM((ROWS, ROWS), BF16),
        ),
        in_specs=[hbm] * 6,
        out_specs=(vmem,) * 4,
        scratch_shapes=[
            pltpu.VMEM((MEM, LAST, COLS, VERT), BF16),
            pltpu.VMEM((MEM, NBLK, OBS), BF16),
            pltpu.VMEM((NBLK, OBS), F32),
            pltpu.VMEM((NBLK, OBS), BF16),
            pltpu.SMEM((NBLK,), jnp.int32),
            pltpu.SMEM((NBLK,), jnp.int32),
            pltpu.VMEM((OBS // 128, MEM * NBLK, 128), F32),
            pltpu.VMEM((LAST, ROWS, ROWS), BF16),
            pltpu.VMEM((MEM, ROWS), BF16),
            pltpu.VMEM((NBLK, MEM, MEM), F32),
            pltpu.VMEM((NBLK, MEM, MEM), F32),
            pltpu.VMEM((NBLK, MEM, MEM), F32),
            pltpu.VMEM((NBLK, 8, 128), F32),
            pltpu.VMEM((NBLK, MEM, MEM), BF16),
            pltpu.VMEM((NGRP, CAP, MEM, MEM), BF16),
            pltpu.VMEM((NGRP, CAP, MEM, MEM), BF16),
            pltpu.VMEM((NGRP, NBLK, 128), jnp.int32),
            pltpu.VMEM((NBLK, 128), jnp.int32),
            dma((2,)), dma((NBLK,)), dma, dma,
            dma((NGRP,)), dma((NGRP,)), dma((NGRP,)), dma((NGRP,)), dma((2,)), dma, dma((4,)),
        ],
        compiler_params=pltpu.CompilerParams(
            collective_id=0, has_side_effects=True, vmem_limit_bytes=46 << 20),
        name="analyse",
    )(prior, equiv, datum, winv, tally, table)
    return pl.pallas_call(
        store_kernel,
        out_shape=(
            jax.ShapeDtypeStruct((MEM, NBLK, COLS, VERT), BF16),
            jax.ShapeDtypeStruct((NBLK, MEM, MEM), BF16),
        ),
        in_specs=[vmem] * 4,
        out_specs=(hbm, hbm),
        scratch_shapes=[pltpu.VMEM((MEM, 1, COLS, VERT), BF16), dma((PARTS + 2,))],
        compiler_params=pltpu.CompilerParams(vmem_limit_bytes=40 << 20),
        name="store",
    )(*made)


def solution(mesh):
    return jax.shard_map(
        body,
        mesh=mesh,
        in_specs=(
            P("mem", "grp", None, None),
            P("mem", "grp", None),
            P(("grp", "mem"), None),
            P(("grp", "mem"), None),
            P(("grp", "mem")),
            P(("grp", "mem")),
        ),
        out_specs=(P(None, ("grp", "mem"), None, None), P(("grp", "mem"), None, None)),
        check_vma=False,
    )
```

```python
import functools
import math

import jax
import jax.numpy as jnp
from jax import lax
from jax.experimental import pallas as pl
from jax.experimental.pallas import tpu as pltpu
from jax.sharding import PartitionSpec as P

ITERS = 12
MEM = 128
NBLK = 8
COLS = 8
VERT = 512
OBS = 1024
NGRP = 4
NMEM = 32
OWN = MEM // NMEM
CAP = NBLK // 2
LAST = NBLK - 1
HALF = OWN // 2
PARTS = 4
STEP = MEM // PARTS
ROWS = MEM * COLS
MESH = pl.DeviceIdType.MESH
HIGH = lax.Precision.HIGHEST
F32 = jnp.float32
BF16 = jnp.bfloat16


def mm(a, b):
    return jnp.dot(a, b, precision=HIGH, preferred_element_type=F32)


def analysis_kernel(
    prior, equiv, datum_hbm, winv_hbm, tally_hbm, table_hbm,
    out, slots, xlast, klast,
    xg, yg, datum, winv, tally, table, yf, kron, spread, ymat, zmat, pmat, scales, wts, pack, got, tabs, tab_mine,
    x_send, x_recv, y_send, y_recv, g_send, g_recv, t_send, t_recv, x_loc, y_loc, s_loc,
):
    g = lax.axis_index("grp")
    m = lax.axis_index("mem")
    row, col, core = m // 8, (m // 2) % 4, m % 2

    def peer(i):
        return (((row + i // 8) % 4) * 4 + (col + (i // 2) % 4) % 4) * 2 + (core + i % 2) % 2

    rows = [lax.rem(row + d, 4) * 8 for d in range(4)]
    cols = [lax.rem(col + d, 4) * 2 for d in range(4)]
    cores = [core, 1 - core]
    peers = [rows[i // 8] + cols[(i // 2) % 4] + cores[i % 2] for i in range(NMEM)]

    barrier = pltpu.get_barrier_semaphore()

    for i in range(1, NMEM):
        pl.semaphore_signal(barrier, inc=1, device_id=(g, peers[i]), device_id_type=MESH)
    for d in range(1, NGRP):
        pl.semaphore_signal(barrier, inc=1, device_id=((g + d) % NGRP, m), device_id_type=MESH)
    pl.semaphore_wait(barrier, NMEM - 1 + NGRP - 1)

    def send_obs(i, carry):
        p = peer((i % (NMEM - 1) + 1) * 5 % NMEM)
        part = i // (NMEM - 1)
        pltpu.make_async_remote_copy(
            src_ref=equiv.at[pl.ds(part, 1), p], dst_ref=yg.at[pl.ds(OWN * m + part, 1)],
            send_sem=y_send, recv_sem=y_recv, device_id=(g, p), device_id_type=MESH,
        ).start()
        return carry

    lax.fori_loop(0, OWN * (NMEM - 1), send_obs, 0)
    own_y = pltpu.make_async_copy(equiv.at[:, m], yg.at[pl.ds(OWN * m, OWN)], y_loc)
    own_y.start()

    small = [
        pltpu.make_async_copy(a, b, s_loc.at[n])
        for n, (a, b) in enumerate(
            ((datum_hbm, datum), (winv_hbm, winv), (tally_hbm, tally), (table_hbm, table)))
    ]
    for c in small:
        c.start()

    def send_block(q, land, sem):
        def send_prior(i, inner):
            p = peer((i % (NMEM - 1) + 1) * 5 % NMEM)
            part = HALF * (i // (NMEM - 1))
            pltpu.make_async_remote_copy(
                src_ref=prior.at[pl.ds(part, HALF), pl.ds(NBLK * p + q, 1)],
                dst_ref=land(pl.ds(OWN * m + part, HALF)),
                send_sem=sem, recv_sem=x_recv.at[q], device_id=(g, p), device_id_type=MESH,
            ).start()
            return inner

        return lax.fori_loop(0, OWN // HALF * (NMEM - 1), send_prior, 0)

    def send_early(q, carry):
        send_block(q, lambda rows: xg.at[rows, pl.ds(q, 1)], x_send.at[0])
        return carry

    lax.fori_loop(0, LAST, send_early, 0)
    far = sorted(range(1, NMEM), key=lambda i: -(min(i // 8, 4 - i // 8) + min((i // 2) % 4, 4 - (i // 2) % 4)))
    for i in far:
        for part in range(0, OWN, HALF):
            p = peers[i]
            pltpu.make_async_remote_copy(
                src_ref=prior.at[pl.ds(part, HALF), pl.ds(NBLK * p + LAST, 1)],
                dst_ref=xlast.at[pl.ds(OWN * m + part, HALF)],
                send_sem=x_send.at[1], recv_sem=x_recv.at[LAST], device_id=(g, p), device_id_type=MESH,
            ).start()
    own_x = [
        pltpu.make_async_copy(
            prior.at[:, pl.ds(NBLK * m, LAST)], xg.at[pl.ds(OWN * m, OWN)], x_loc.at[0]),
        pltpu.make_async_copy(
            prior.at[:, pl.ds(NBLK * m + LAST, 1)], xlast.at[pl.ds(OWN * m, OWN)], x_loc.at[1]),
    ]
    for c in own_x:
        c.start()

    for c in small:
        c.wait()

    for j in range(NBLK):
        tab_mine[j:j + 1, :] = jnp.full((1, 128), table[j], jnp.int32)
    tab_copies = []
    for d in range(1, NGRP):
        c = pltpu.make_async_remote_copy(
            src_ref=tab_mine, dst_ref=tabs.at[g],
            send_sem=t_send.at[d], recv_sem=t_recv.at[d],
            device_id=((g + d) % NGRP, m), device_id_type=MESH)
        c.start()
        tab_copies.append(c)

    spread[...] = (
        lax.broadcasted_iota(jnp.int32, (MEM, ROWS), 0)
        == lax.broadcasted_iota(jnp.int32, (MEM, ROWS), 1) // COLS
    ).astype(F32).astype(BF16)
    eye = (
        lax.broadcasted_iota(jnp.int32, (MEM, MEM), 0)
        == lax.broadcasted_iota(jnp.int32, (MEM, MEM), 1)
    ).astype(F32)

    own_y.wait()
    landed = yg.at[pl.ds(0, MEM - OWN)]
    pltpu.make_async_copy(landed, landed, y_recv).wait()

    def add_member(k, acc):
        return acc + yg[k].astype(F32)

    total = lax.fori_loop(0, MEM, add_member, jnp.zeros((NBLK, OBS), F32))
    ybar = total * (1.0 / MEM)
    yf_mean = ybar

    def take_mean(k, carry):
        d = (yg[k].astype(F32) - yf_mean).astype(BF16).astype(F32)
        for ch in range(OBS // 128):
            yf[ch, pl.ds(pl.multiple_of(k * NBLK, NBLK), NBLK), :] = d[:, ch * 128:(ch + 1) * 128]
        return carry

    lax.fori_loop(0, MEM, take_mean, 0)
    innov = (datum[...] - ybar).astype(BF16).astype(F32)
    rinv = winv[...].astype(F32)
    for b in range(NBLK):
        live = lax.broadcasted_iota(jnp.int32, (1, OBS), 1) < tally[b]
        rmask = jnp.where(live, rinv[b:b + 1, :], 0.0)
        yp = jnp.concatenate(
            [yf[ch, pl.ds(b, MEM, stride=NBLK), :] for ch in range(OBS // 128)], axis=1)
        yr = (yp * rmask).astype(BF16)
        both = jnp.concatenate(
            [yp.astype(BF16), jnp.broadcast_to(innov[b:b + 1, :], (MEM, OBS)).astype(BF16)], axis=0)
        prod = lax.dot_general(yr, both, (((1,), (1,)), ((), ())), preferred_element_type=F32)
        amat = (MEM - 1.0) * eye + prod[:, :MEM]
        pmat[b] = prod[:, MEM:]
        scale = jnp.sqrt(jnp.sum(jnp.sum(amat * amat, axis=1, keepdims=True), axis=0, keepdims=True))
        scales[b] = jnp.broadcast_to(scale, (8, 128))
        ymat[b] = amat / scale
        zmat[b] = eye

    def newton(it, carry):
        ts = [1.5 * eye - 0.5 * mm(zmat[b], ymat[b]) for b in range(NBLK)]
        for b in range(NBLK):
            ymat[b] = mm(ymat[b], ts[b])
            zmat[b] = mm(ts[b], zmat[b])
        return carry

    lax.fori_loop(0, ITERS, newton, 0)

    for b in range(NBLK):
        root = zmat[b] / jnp.sqrt(scales[b][:1])
        wmean = mm(root, mm(root, pmat[b]))
        full = math.sqrt(MEM - 1.0) * root + wmean
        full = full + (1.0 - jnp.sum(full, axis=0, keepdims=True)) / MEM
        wts[b] = full.astype(BF16)

    within = []
    for j in range(NBLK):
        n = jnp.int32(0)
        for k in range(j):
            n = n + (table[k] == table[j]).astype(jnp.int32)
        within.append(n)
    for t in range(NGRP):
        for w in range(CAP):
            src = jnp.int32(0)
            for j in range(NBLK):
                src = src + jnp.int32(j) * ((table[j] == t) & (within[j] == w)).astype(jnp.int32)
            pack[t, w] = wts[src]
    w_copies = []
    for d in range(1, NGRP):
        to = (g + d) % NGRP
        c = pltpu.make_async_remote_copy(
            src_ref=pack.at[to], dst_ref=got.at[g],
            send_sem=g_send.at[d], recv_sem=g_recv.at[d],
            device_id=(to, m), device_id_type=MESH)
        c.start()
        w_copies.append(c)

    mask = (
        lax.broadcasted_iota(jnp.int32, (COLS, ROWS), 0)
        == lax.broadcasted_iota(jnp.int32, (COLS, ROWS), 1) % COLS
    ).astype(F32)

    def expanded(b):
        wide = lax.dot_general(
            wts[b], spread[...], (((0,), (0,)), ((), ())), preferred_element_type=F32)
        return (wide[:, None, :] * mask[None]).reshape(ROWS, ROWS).astype(BF16)

    def expand(b, carry):
        kron[b] = expanded(b)
        return carry

    lax.fori_loop(0, LAST, expand, 0)
    klast[...] = expanded(LAST)

    for c in tab_copies:
        c.wait()
    for c in w_copies:
        c.wait()
    tabs[g] = tab_mine[...]
    got[g] = pack[g]
    base = jnp.zeros((1, 128), jnp.int32)
    ranks = []
    for gg in range(NGRP):
        hits = tabs[gg] == g
        count = jnp.sum(hits.astype(F32), axis=0, keepdims=True).astype(jnp.int32)
        for w in range(CAP):
            ranks.append(jnp.where(count > w, base + w, -1))
        base = base + count
    for k in range(NBLK):
        acc = jnp.zeros((MEM, MEM), F32)
        for gg in range(NGRP):
            for w in range(CAP):
                acc = jnp.where(ranks[gg * CAP + w] == k, got[gg, w].astype(F32), acc)
        slots[k] = acc.astype(BF16)

    for c in own_x:
        c.wait()

    def mix(q, carry):
        here = xg.at[pl.ds(0, MEM - OWN), pl.ds(q, 1)]
        pltpu.make_async_copy(here, here, x_recv.at[q]).wait()
        state = xg[:, q].astype(F32).reshape(ROWS, VERT).astype(BF16)
        for part in range(PARTS):
            out[part * STEP:(part + 1) * STEP, q] = mixed(kron.at[q], state, part)
        return carry

    lax.fori_loop(0, LAST, mix, 0)
    here = xlast.at[pl.ds(0, MEM - OWN)]
    pltpu.make_async_copy(here, here, x_recv.at[LAST]).wait()

    sent = yg.at[pl.ds(0, MEM - OWN)]
    pltpu.make_async_copy(sent, sent, y_send).wait()
    sent = xg.at[pl.ds(0, MEM - OWN)]
    pltpu.make_async_copy(sent, sent, x_send.at[0]).wait()
    sent = xlast.at[pl.ds(0, MEM - OWN)]
    pltpu.make_async_copy(sent, sent, x_send.at[1]).wait()


def mixed(weights, state, part):
    rows = weights[part * STEP * COLS:(part + 1) * STEP * COLS, :]
    total = jnp.dot(rows, state, preferred_element_type=F32)
    return total.reshape(STEP, COLS, VERT).astype(BF16)


def store_kernel(analysis, slots, xlast, klast, out, out_slots, made, sems):
    copies = [
        pltpu.make_async_copy(analysis, out.at[:, pl.ds(0, LAST)], sems.at[PARTS]),
        pltpu.make_async_copy(slots, out_slots, sems.at[PARTS + 1]),
    ]
    for c in copies:
        c.start()
    state = xlast[:, 0].astype(F32).reshape(ROWS, VERT).astype(BF16)
    for part in range(PARTS):
        rows = pl.ds(part * STEP, STEP)
        made[rows, 0] = mixed(klast, state, part)
        c = pltpu.make_async_copy(made.at[rows], out.at[rows, pl.ds(LAST, 1)], sems.at[part])
        c.start()
        copies.append(c)
    for c in copies:
        c.wait()


def body(prior, equiv, datum, winv, tally, table):
    vmem = pl.BlockSpec(memory_space=pltpu.VMEM)
    hbm = pl.BlockSpec(memory_space=pltpu.HBM)
    dma = pltpu.SemaphoreType.DMA
    equiv = equiv.reshape(OWN, NMEM, NBLK, OBS)
    made = pl.pallas_call(
        analysis_kernel,
        out_shape=(
            pltpu.VMEM((MEM, LAST, COLS, VERT), BF16),
            pltpu.VMEM((NBLK, MEM, MEM), BF16),
            pltpu.VMEM((MEM, 1, COLS, VERT), BF16),
            pltpu.VMEM((ROWS, ROWS), BF16),
        ),
        in_specs=[hbm] * 6,
        out_specs=(vmem,) * 4,
        scratch_shapes=[
            pltpu.VMEM((MEM, LAST, COLS, VERT), BF16),
            pltpu.VMEM((MEM, NBLK, OBS), BF16),
            pltpu.VMEM((NBLK, OBS), F32),
            pltpu.VMEM((NBLK, OBS), BF16),
            pltpu.SMEM((NBLK,), jnp.int32),
            pltpu.SMEM((NBLK,), jnp.int32),
            pltpu.VMEM((OBS // 128, MEM * NBLK, 128), F32),
            pltpu.VMEM((LAST, ROWS, ROWS), BF16),
            pltpu.VMEM((MEM, ROWS), BF16),
            pltpu.VMEM((NBLK, MEM, MEM), F32),
            pltpu.VMEM((NBLK, MEM, MEM), F32),
            pltpu.VMEM((NBLK, MEM, MEM), F32),
            pltpu.VMEM((NBLK, 8, 128), F32),
            pltpu.VMEM((NBLK, MEM, MEM), BF16),
            pltpu.VMEM((NGRP, CAP, MEM, MEM), BF16),
            pltpu.VMEM((NGRP, CAP, MEM, MEM), BF16),
            pltpu.VMEM((NGRP, NBLK, 128), jnp.int32),
            pltpu.VMEM((NBLK, 128), jnp.int32),
            dma((2,)), dma((NBLK,)), dma, dma,
            dma((NGRP,)), dma((NGRP,)), dma((NGRP,)), dma((NGRP,)), dma((2,)), dma, dma((4,)),
        ],
        compiler_params=pltpu.CompilerParams(
            collective_id=0, has_side_effects=True, vmem_limit_bytes=46 << 20),
        name="analyse",
    )(prior, equiv, datum, winv, tally, table)
    return pl.pallas_call(
        store_kernel,
        out_shape=(
            jax.ShapeDtypeStruct((MEM, NBLK, COLS, VERT), BF16),
            jax.ShapeDtypeStruct((NBLK, MEM, MEM), BF16),
        ),
        in_specs=[vmem] * 4,
        out_specs=(hbm, hbm),
        scratch_shapes=[pltpu.VMEM((MEM, 1, COLS, VERT), BF16), dma((PARTS + 2,))],
        compiler_params=pltpu.CompilerParams(vmem_limit_bytes=40 << 20),
        name="store",
    )(*made)


def solution(mesh):
    return jax.shard_map(
        body,
        mesh=mesh,
        in_specs=(
            P("mem", "grp", None, None),
            P("mem", "grp", None),
            P(("grp", "mem"), None),
            P(("grp", "mem"), None),
            P(("grp", "mem")),
            P(("grp", "mem")),
        ),
        out_specs=(P(None, ("grp", "mem"), None, None), P(("grp", "mem"), None, None)),
        check_vma=False,
    )
```

```python
import functools
import math

import jax
import jax.numpy as jnp
from jax import lax
from jax.experimental import pallas as pl
from jax.experimental.pallas import tpu as pltpu
from jax.sharding import PartitionSpec as P

ITERS = 12
MEM = 128
NBLK = 8
COLS = 8
VERT = 512
OBS = 1024
NGRP = 4
NMEM = 32
OWN = MEM // NMEM
CAP = NBLK // 2
LAST = NBLK - 1
HALF = OWN // 2
PARTS = 4
STEP = MEM // PARTS
ROWS = MEM * COLS
MESH = pl.DeviceIdType.MESH
HIGH = lax.Precision.HIGHEST
F32 = jnp.float32
BF16 = jnp.bfloat16


def mm(a, b):
    return jnp.dot(a, b, precision=HIGH, preferred_element_type=F32)


def analysis_kernel(
    prior, equiv, datum_hbm, winv_hbm, tally_hbm, table_hbm,
    out, slots, xlast, klast,
    xg, yg, datum, winv, tally, table, yf, kron, spread, ymat, zmat, pmat, scales, wts, pack, got, tabs, tab_mine,
    x_send, x_recv, y_send, y_recv, g_send, g_recv, t_send, t_recv, x_loc, y_loc, s_loc,
):
    g = lax.axis_index("grp")
    m = lax.axis_index("mem")
    row, col, core = m // 8, (m // 2) % 4, m % 2

    def peer(i):
        return (((row + i // 8) % 4) * 4 + (col + (i // 2) % 4) % 4) * 2 + (core + i % 2) % 2

    rows = [lax.rem(row + d, 4) * 8 for d in range(4)]
    cols = [lax.rem(col + d, 4) * 2 for d in range(4)]
    cores = [core, 1 - core]
    peers = [rows[i // 8] + cols[(i // 2) % 4] + cores[i % 2] for i in range(NMEM)]

    far = sorted(range(1, NMEM), key=lambda i: -(min(i // 8, 4 - i // 8) + min((i // 2) % 4, 4 - (i // 2) % 4)))

    barrier = pltpu.get_barrier_semaphore()

    for i in far:
        pl.semaphore_signal(barrier, inc=1, device_id=(g, peers[i]), device_id_type=MESH)
    for d in range(1, NGRP):
        pl.semaphore_signal(barrier, inc=1, device_id=((g + d) % NGRP, m), device_id_type=MESH)
    pl.semaphore_wait(barrier, NMEM - 1 + NGRP - 1)

    def send_obs(i, carry):
        p = peer((i % (NMEM - 1) + 1) * 5 % NMEM)
        part = i // (NMEM - 1)
        pltpu.make_async_remote_copy(
            src_ref=equiv.at[pl.ds(part, 1), p], dst_ref=yg.at[pl.ds(OWN * m + part, 1)],
            send_sem=y_send, recv_sem=y_recv, device_id=(g, p), device_id_type=MESH,
        ).start()
        return carry

    lax.fori_loop(0, OWN * (NMEM - 1), send_obs, 0)
    own_y = pltpu.make_async_copy(equiv.at[:, m], yg.at[pl.ds(OWN * m, OWN)], y_loc)
    own_y.start()

    small = [
        pltpu.make_async_copy(a, b, s_loc.at[n])
        for n, (a, b) in enumerate(
            ((datum_hbm, datum), (winv_hbm, winv), (tally_hbm, tally), (table_hbm, table)))
    ]
    for c in small:
        c.start()

    def send_block(q, land, sem):
        def send_prior(i, inner):
            p = peer((i % (NMEM - 1) + 1) * 5 % NMEM)
            part = HALF * (i // (NMEM - 1))
            pltpu.make_async_remote_copy(
                src_ref=prior.at[pl.ds(part, HALF), pl.ds(NBLK * p + q, 1)],
                dst_ref=land(pl.ds(OWN * m + part, HALF)),
                send_sem=sem, recv_sem=x_recv.at[q], device_id=(g, p), device_id_type=MESH,
            ).start()
            return inner

        return lax.fori_loop(0, OWN // HALF * (NMEM - 1), send_prior, 0)

    def send_early(q, carry):
        send_block(q, lambda rows: xg.at[rows, pl.ds(q, 1)], x_send.at[0])
        return carry

    lax.fori_loop(0, LAST, send_early, 0)
    for i in far[-1:] + far[:-1]:
        for part in range(0, OWN, HALF):
            p = peers[i]
            pltpu.make_async_remote_copy(
                src_ref=prior.at[pl.ds(part, HALF), pl.ds(NBLK * p + LAST, 1)],
                dst_ref=xlast.at[pl.ds(OWN * m + part, HALF)],
                send_sem=x_send.at[1], recv_sem=x_recv.at[LAST], device_id=(g, p), device_id_type=MESH,
            ).start()
    own_x = [
        pltpu.make_async_copy(
            prior.at[:, pl.ds(NBLK * m, LAST)], xg.at[pl.ds(OWN * m, OWN)], x_loc.at[0]),
        pltpu.make_async_copy(
            prior.at[:, pl.ds(NBLK * m + LAST, 1)], xlast.at[pl.ds(OWN * m, OWN)], x_loc.at[1]),
    ]
    for c in own_x:
        c.start()

    for c in small:
        c.wait()

    for j in range(NBLK):
        tab_mine[j:j + 1, :] = jnp.full((1, 128), table[j], jnp.int32)
    tab_copies = []
    for d in range(1, NGRP):
        c = pltpu.make_async_remote_copy(
            src_ref=tab_mine, dst_ref=tabs.at[g],
            send_sem=t_send.at[d], recv_sem=t_recv.at[d],
            device_id=((g + d) % NGRP, m), device_id_type=MESH)
        c.start()
        tab_copies.append(c)

    spread[...] = (
        lax.broadcasted_iota(jnp.int32, (MEM, ROWS), 0)
        == lax.broadcasted_iota(jnp.int32, (MEM, ROWS), 1) // COLS
    ).astype(F32).astype(BF16)
    eye = (
        lax.broadcasted_iota(jnp.int32, (MEM, MEM), 0)
        == lax.broadcasted_iota(jnp.int32, (MEM, MEM), 1)
    ).astype(F32)

    own_y.wait()
    landed = yg.at[pl.ds(0, MEM - OWN)]
    pltpu.make_async_copy(landed, landed, y_recv).wait()

    def add_member(k, acc):
        return acc + yg[k].astype(F32)

    total = lax.fori_loop(0, MEM, add_member, jnp.zeros((NBLK, OBS), F32))
    ybar = total * (1.0 / MEM)
    yf_mean = ybar

    def take_mean(k, carry):
        d = (yg[k].astype(F32) - yf_mean).astype(BF16).astype(F32)
        for ch in range(OBS // 128):
            yf[ch, pl.ds(pl.multiple_of(k * NBLK, NBLK), NBLK), :] = d[:, ch * 128:(ch + 1) * 128]
        return carry

    lax.fori_loop(0, MEM, take_mean, 0)
    innov = (datum[...] - ybar).astype(BF16).astype(F32)
    rinv = winv[...].astype(F32)
    for b in range(NBLK):
        live = lax.broadcasted_iota(jnp.int32, (1, OBS), 1) < tally[b]
        rmask = jnp.where(live, rinv[b:b + 1, :], 0.0)
        yp = jnp.concatenate(
            [yf[ch, pl.ds(b, MEM, stride=NBLK), :] for ch in range(OBS // 128)], axis=1)
        yr = (yp * rmask).astype(BF16)
        both = jnp.concatenate(
            [yp.astype(BF16), jnp.broadcast_to(innov[b:b + 1, :], (MEM, OBS)).astype(BF16)], axis=0)
        prod = lax.dot_general(yr, both, (((1,), (1,)), ((), ())), preferred_element_type=F32)
        amat = (MEM - 1.0) * eye + prod[:, :MEM]
        pmat[b] = prod[:, MEM:]
        scale = jnp.sqrt(jnp.sum(jnp.sum(amat * amat, axis=1, keepdims=True), axis=0, keepdims=True))
        scales[b] = jnp.broadcast_to(scale, (8, 128))
        ymat[b] = amat / scale
        zmat[b] = eye

    def newton(it, carry):
        ts = [1.5 * eye - 0.5 * mm(zmat[b], ymat[b]) for b in range(NBLK)]
        for b in range(NBLK):
            ymat[b] = mm(ymat[b], ts[b])
            zmat[b] = mm(ts[b], zmat[b])
        return carry

    lax.fori_loop(0, ITERS, newton, 0)

    for b in range(NBLK):
        root = zmat[b] / jnp.sqrt(scales[b][:1])
        wmean = mm(root, mm(root, pmat[b]))
        full = math.sqrt(MEM - 1.0) * root + wmean
        full = full + (1.0 - jnp.sum(full, axis=0, keepdims=True)) / MEM
        wts[b] = full.astype(BF16)

    within = []
    for j in range(NBLK):
        n = jnp.int32(0)
        for k in range(j):
            n = n + (table[k] == table[j]).astype(jnp.int32)
        within.append(n)
    for t in range(NGRP):
        for w in range(CAP):
            src = jnp.int32(0)
            for j in range(NBLK):
                src = src + jnp.int32(j) * ((table[j] == t) & (within[j] == w)).astype(jnp.int32)
            pack[t, w] = wts[src]
    w_copies = []
    for d in range(1, NGRP):
        to = (g + d) % NGRP
        c = pltpu.make_async_remote_copy(
            src_ref=pack.at[to], dst_ref=got.at[g],
            send_sem=g_send.at[d], recv_sem=g_recv.at[d],
            device_id=(to, m), device_id_type=MESH)
        c.start()
        w_copies.append(c)

    mask = (
        lax.broadcasted_iota(jnp.int32, (COLS, ROWS), 0)
        == lax.broadcasted_iota(jnp.int32, (COLS, ROWS), 1) % COLS
    ).astype(F32)

    def expanded(b):
        wide = lax.dot_general(
            wts[b], spread[...], (((0,), (0,)), ((), ())), preferred_element_type=F32)
        return (wide[:, None, :] * mask[None]).reshape(ROWS, ROWS).astype(BF16)

    def expand(b, carry):
        kron[b] = expanded(b)
        return carry

    lax.fori_loop(0, LAST, expand, 0)
    klast[...] = expanded(LAST)

    for c in tab_copies:
        c.wait()
    for c in w_copies:
        c.wait()
    tabs[g] = tab_mine[...]
    got[g] = pack[g]
    base = jnp.zeros((1, 128), jnp.int32)
    ranks = []
    for gg in range(NGRP):
        hits = tabs[gg] == g
        count = jnp.sum(hits.astype(F32), axis=0, keepdims=True).astype(jnp.int32)
        for w in range(CAP):
            ranks.append(jnp.where(count > w, base + w, -1))
        base = base + count
    for k in range(NBLK):
        acc = jnp.zeros((MEM, MEM), F32)
        for gg in range(NGRP):
            for w in range(CAP):
                acc = jnp.where(ranks[gg * CAP + w] == k, got[gg, w].astype(F32), acc)
        slots[k] = acc.astype(BF16)

    for c in own_x:
        c.wait()

    def mix(q, carry):
        here = xg.at[pl.ds(0, MEM - OWN), pl.ds(q, 1)]
        pltpu.make_async_copy(here, here, x_recv.at[q]).wait()
        state = xg[:, q].astype(F32).reshape(ROWS, VERT).astype(BF16)
        for part in range(PARTS):
            out[part * STEP:(part + 1) * STEP, q] = mixed(kron.at[q], state, part)
        return carry

    lax.fori_loop(0, LAST, mix, 0)
    here = xlast.at[pl.ds(0, MEM - OWN)]
    pltpu.make_async_copy(here, here, x_recv.at[LAST]).wait()

    sent = yg.at[pl.ds(0, MEM - OWN)]
    pltpu.make_async_copy(sent, sent, y_send).wait()
    sent = xg.at[pl.ds(0, MEM - OWN)]
    pltpu.make_async_copy(sent, sent, x_send.at[0]).wait()
    sent = xlast.at[pl.ds(0, MEM - OWN)]
    pltpu.make_async_copy(sent, sent, x_send.at[1]).wait()


def mixed(weights, state, part):
    rows = weights[part * STEP * COLS:(part + 1) * STEP * COLS, :]
    total = jnp.dot(rows, state, preferred_element_type=F32)
    return total.reshape(STEP, COLS, VERT).astype(BF16)


def store_kernel(analysis, slots, xlast, klast, out, out_slots, made, sems):
    copies = [
        pltpu.make_async_copy(analysis, out.at[:, pl.ds(0, LAST)], sems.at[PARTS]),
        pltpu.make_async_copy(slots, out_slots, sems.at[PARTS + 1]),
    ]
    for c in copies:
        c.start()
    state = xlast[:, 0].astype(F32).reshape(ROWS, VERT).astype(BF16)
    for part in range(PARTS):
        rows = pl.ds(part * STEP, STEP)
        made[rows, 0] = mixed(klast, state, part)
        c = pltpu.make_async_copy(made.at[rows], out.at[rows, pl.ds(LAST, 1)], sems.at[part])
        c.start()
        copies.append(c)
    for c in copies:
        c.wait()


def body(prior, equiv, datum, winv, tally, table):
    vmem = pl.BlockSpec(memory_space=pltpu.VMEM)
    hbm = pl.BlockSpec(memory_space=pltpu.HBM)
    dma = pltpu.SemaphoreType.DMA
    equiv = equiv.reshape(OWN, NMEM, NBLK, OBS)
    made = pl.pallas_call(
        analysis_kernel,
        out_shape=(
            pltpu.VMEM((MEM, LAST, COLS, VERT), BF16),
            pltpu.VMEM((NBLK, MEM, MEM), BF16),
            pltpu.VMEM((MEM, 1, COLS, VERT), BF16),
            pltpu.VMEM((ROWS, ROWS), BF16),
        ),
        in_specs=[hbm] * 6,
        out_specs=(vmem,) * 4,
        scratch_shapes=[
            pltpu.VMEM((MEM, LAST, COLS, VERT), BF16),
            pltpu.VMEM((MEM, NBLK, OBS), BF16),
            pltpu.VMEM((NBLK, OBS), F32),
            pltpu.VMEM((NBLK, OBS), BF16),
            pltpu.SMEM((NBLK,), jnp.int32),
            pltpu.SMEM((NBLK,), jnp.int32),
            pltpu.VMEM((OBS // 128, MEM * NBLK, 128), F32),
            pltpu.VMEM((LAST, ROWS, ROWS), BF16),
            pltpu.VMEM((MEM, ROWS), BF16),
            pltpu.VMEM((NBLK, MEM, MEM), F32),
            pltpu.VMEM((NBLK, MEM, MEM), F32),
            pltpu.VMEM((NBLK, MEM, MEM), F32),
            pltpu.VMEM((NBLK, 8, 128), F32),
            pltpu.VMEM((NBLK, MEM, MEM), BF16),
            pltpu.VMEM((NGRP, CAP, MEM, MEM), BF16),
            pltpu.VMEM((NGRP, CAP, MEM, MEM), BF16),
            pltpu.VMEM((NGRP, NBLK, 128), jnp.int32),
            pltpu.VMEM((NBLK, 128), jnp.int32),
            dma((2,)), dma((NBLK,)), dma, dma,
            dma((NGRP,)), dma((NGRP,)), dma((NGRP,)), dma((NGRP,)), dma((2,)), dma, dma((4,)),
        ],
        compiler_params=pltpu.CompilerParams(
            collective_id=0, has_side_effects=True, vmem_limit_bytes=46 << 20),
        name="analyse",
    )(prior, equiv, datum, winv, tally, table)
    return pl.pallas_call(
        store_kernel,
        out_shape=(
            jax.ShapeDtypeStruct((MEM, NBLK, COLS, VERT), BF16),
            jax.ShapeDtypeStruct((NBLK, MEM, MEM), BF16),
        ),
        in_specs=[vmem] * 4,
        out_specs=(hbm, hbm),
        scratch_shapes=[pltpu.VMEM((MEM, 1, COLS, VERT), BF16), dma((PARTS + 2,))],
        compiler_params=pltpu.CompilerParams(vmem_limit_bytes=40 << 20),
        name="store",
    )(*made)


def solution(mesh):
    return jax.shard_map(
        body,
        mesh=mesh,
        in_specs=(
            P("mem", "grp", None, None),
            P("mem", "grp", None),
            P(("grp", "mem"), None),
            P(("grp", "mem"), None),
            P(("grp", "mem")),
            P(("grp", "mem")),
        ),
        out_specs=(P(None, ("grp", "mem"), None, None), P(("grp", "mem"), None, None)),
        check_vma=False,
    )
```
